32 devices in a mesh: query: 4 (over x, core), item: 8 (over z, y).
Axes of the slice: x: 2, y: 2, z: 4, core: 2. Of those that a mesh axis runs over, the one named last changes fastest.
Arguments:
- queries: bfloat16 [12288, 1024], P(('query', 'item')), may hold values from -6 to 6
- item_table: bfloat16 [16384, 1024], P('item'), may hold values from -6 to 6
- w_query: bfloat16 [1024, 512], replicated, may hold values from -0.1875 to 0.1875
- w_item_in: bfloat16 [1024, 1024], replicated, may hold values from -0.1875 to 0.1875
- w_item_out: bfloat16 [1024, 512], replicated, may hold values from -0.1875 to 0.1875
- pos_owner: int32 [12288, 1], P(('query', 'item')), may hold values from 0 to 7; in each aligned block of 384 rows (0 to 383, 384 to 767, ...) at most 96 rows name the same one
- pos_rows: int32 [12288], P(('query', 'item')), may hold values from 0 to 2047
- neg_owner: int32 [4, 1024, 1], P('query'), may hold values from 0 to 7; in each aligned block of 1024 rows (0 to 1023, 1024 to 2047, ..., all dimensions but the last counted through in order) at most 256 rows name the same one
- neg_rows: int32 [4, 1024], P('query'), may hold values from 0 to 2047
- neg_logq: float32 [4, 1024], P('query'), may hold values from 7 to 8
Outputs:
- grad_query: float32 [1024, 512], P('item', 'query')
- grad_item_in: float32 [1024, 1024], P('item', 'query')
- grad_item_out: float32 [1024, 512], P('item', 'query')
The draws below stay inside these ranges and needn't reach their ends.
Inputs may be any that keep to these rules, and one draw needn't show every extreme that they name: `pos_owner`: among the 384 rows of one device no owner is named more than 96 times, a bound that some block reaches. `neg_owner`: among the 1024 negatives of one group no owner is named more than 256 times, a bound that some block reaches.
All inputs are finite; a program needn't handle non-finite values.
Results may differ from the reference program's by a relative error of at most 0.0065.
Values may be sent and summed in bfloat16 or wider, within the bound.
A program may use at most 128 MiB of HBM per device.

```python
import math
import jax
import jax.numpy as jnp
import numpy as np
from jax import lax

QF = 1024
F = 1024
H = 1024
E = 512
Q_DEV = 384
ITEMS_DEV = 2048
GROUPS = 4
QUERIES = 12288
NEG = 1024
CAP = 256
PCAP = 96
ITEMS = 16384
N_ITEM = 8


def place_ends(array, stream_key, low, high):
    shape = array.shape
    spot = [jax.random.randint(jax.random.fold_in(stream_key, axis), (), 0, shape[axis]) for axis in range(len(shape))]
    array = array.at[tuple(spot)].set(low)
    longest = shape.index(max(shape))
    spot[longest] = (spot[longest] + 1) % shape[longest]
    return array.at[tuple(spot)].set(high)


def spiked(result, own_key, source, target, parts, factor):
    def block_of(axis_at):
        return (jnp.arange(result.shape[axis_at]) // (result.shape[axis_at] // parts)).reshape((-1,) + (1,) * (result.ndim - 1 - axis_at))

    first = jax.random.permutation(own_key, parts)[block_of(target)]
    second = (block_of(target) + parts // 2) % parts
    return jnp.where((block_of(source) == first) | (block_of(source) == second), factor * result, result)


def block_scale(stream_key, dims, pieces, smallest, high):
    loudness = 1.0
    for axis_at, blocks in pieces:
        draws = jax.random.uniform(jax.random.fold_in(jax.random.fold_in(stream_key, 6), axis_at), (blocks,), jnp.float32, smallest / len(pieces), high / len(pieces))
        loudness = loudness * jnp.repeat(jnp.exp(draws), dims[axis_at] // blocks).reshape((-1,) + (1,) * (len(dims) - 1 - axis_at))
    return loudness


def deal_out(own_key, own, number, rows, count, top, reach, slope):
    sequence = jax.random.permutation(own_key, count)
    heavy_load, ordinary = portions_of(count, rows * top, reach, slope, True), portions_of(count, rows * top, reach, slope, False)
    places = jnp.arange(count)

    def named(tallies, turn):
        used = int((tallies > 0).sum())
        fixed = max(1, used // 4)
        moved = fixed + (places - fixed + turn * (used - fixed)) % max(1, count - fixed)
        return jnp.zeros((count,), jnp.int32).at[sequence[jnp.where(places < fixed, places, moved)]].set(jnp.asarray(tallies, jnp.int32))

    tallies = jnp.where(number % 4 == 0, named(heavy_load, number // 4), named(ordinary, number - number // 4 - 1))
    mixed = jax.random.permutation(jax.random.fold_in(own, 3), count)
    donor, receiver = mixed[0:count // 2 * 2:2], mixed[1:count // 2 * 2:2]
    slack = jnp.minimum(tallies[donor] - 1, reach - tallies[receiver]) // 2
    slack = jnp.where((donor == sequence[0]) | (receiver == sequence[0]) | (tallies[receiver] == 0), 0, jnp.maximum(slack, 0))
    moved = jax.random.randint(jax.random.fold_in(own, 4), (count // 2,), 0, 1 << 20) % (slack + 1)
    tallies = tallies.at[donor].add(-moved).at[receiver].add(moved)
    labels = jnp.searchsorted(jnp.cumsum(tallies), jnp.arange(rows * top), side="right").astype(jnp.int32)
    grid = labels.reshape(top, rows).T
    grid = grid[jax.random.permutation(jax.random.fold_in(own, 1), rows)]
    turn = jax.random.randint(jax.random.fold_in(own, 2), (rows, 1), 0, top)
    return jnp.take_along_axis(grid, (jnp.arange(top)[None, :] + turn) % top, axis=1)


def portions_of(count, total, bound, slope, full):
    portions = [(1 << 20) // math.isqrt(grade ** slope) + 1 for grade in range(1, count + 1)]
    largest = bound if full else min(bound, max(-(-total // count), total * portions[0] // sum(portions)))
    least = 1 if total - largest >= count - 1 else 0
    counts, surplus = [largest] + [least] * (count - 1), total - largest - least * (count - 1)
    while surplus > 0:
        free = [i for i in range(1, count) if counts[i] < largest] or [i for i in range(1, count) if counts[i] < bound]
        pool, left = sum([portions[i] for i in free]), surplus
        for i in free:
            addition = min(bound - counts[i], max(1, left * portions[i] // pool), surplus)
            counts[i] = counts[i] + addition
            surplus = surplus - addition
    return np.array(counts)


def noise(key, shape, spread, limit, shards=(), held_as=jnp.bfloat16):
    array = jax.random.normal(key, shape, jnp.float32) * spread
    if len(shards) > 0:
        array = block_scale(key, shape, shards, -0.22, 0.18) * array
    return jnp.clip(array, min=-limit, max=limit).astype(held_as)


def noise_with(rng, extent, deviation, bound, pieces, heavy, dtype=jnp.bfloat16):
    drawn = deviation * jax.random.normal(rng, extent, jnp.float32)
    if pieces:
        drawn = drawn * block_scale(rng, extent, pieces, -0.22, 0.18)
    return jnp.clip(spiked(drawn, jax.random.fold_in(rng, 3), *heavy), -bound, bound).astype(dtype)


def setup_inputs(seed: int = 0) -> dict:
    keys = jax.random.split(jax.random.key(seed), 11)
    queries = noise_with(keys[0], (QUERIES, QF), 1.0, 6.0, ((0, 32),), (0, 1, 32, 2.75))
    item_table = noise(keys[1], (ITEMS, F), 1.0, 6.0, ((0, 8),))
    w_query = noise(keys[2], (QF, E), QF ** -0.5, 0.1875)
    w_item_in = noise(keys[3], (F, H), F ** -0.5, 0.1875)
    w_item_out = noise(keys[4], (H, E), H ** -0.5, 0.1875)
    pos_owner_keys = jax.random.split(jax.random.fold_in(keys[5], 1), QUERIES // Q_DEV)
    pos_owner_turns = jax.random.permutation(jax.random.fold_in(keys[5], 3), QUERIES // Q_DEV)
    pos_owner = jax.vmap(lambda own, number: deal_out(jax.random.fold_in(keys[5], 2), own, number, Q_DEV, N_ITEM, 1, PCAP, 1))(pos_owner_keys, pos_owner_turns).reshape((QUERIES, 1))
    pos_rows = place_ends(jax.random.randint(keys[6], (QUERIES,), 0, ITEMS_DEV), jax.random.fold_in(keys[6], 1), 0, ITEMS_DEV - 1).astype(jnp.int32)
    neg_owner_keys = jax.random.split(jax.random.fold_in(keys[7], 1), GROUPS * NEG // NEG)
    neg_owner_turns = jax.random.permutation(jax.random.fold_in(keys[7], 3), GROUPS * NEG // NEG)
    neg_owner = jax.vmap(lambda own, number: deal_out(jax.random.fold_in(keys[7], 2), own, number, NEG, N_ITEM, 1, CAP, 2))(neg_owner_keys, neg_owner_turns).reshape((GROUPS, NEG, 1))
    neg_rows = place_ends(jax.random.randint(keys[8], (GROUPS, NEG), 0, ITEMS_DEV), jax.random.fold_in(keys[8], 1), 0, ITEMS_DEV - 1).astype(jnp.int32)
    neg_logq = jnp.clip(7.0 + 1.0 * jax.random.uniform(keys[9], (GROUPS, NEG), jnp.float32) ** block_scale(keys[9], (GROUPS, NEG), ((0, 4),), -0.2, 0.2), 7.0, 8.0)
    return {"queries": queries, "item_table": item_table, "w_query": w_query, "w_item_in": w_item_in, "w_item_out": w_item_out, "pos_owner": pos_owner, "pos_rows": pos_rows, "neg_owner": neg_owner, "neg_rows": neg_rows, "neg_logq": neg_logq}


TAU = 0.02
EPS = 1e-06

def item_tower(features, w_item_in, w_item_out):
    hidden_pre = jnp.dot(features, w_item_in, preferred_element_type=jnp.float32)
    hidden = jax.nn.silu(hidden_pre).astype(jnp.bfloat16)
    output = jnp.dot(hidden, w_item_out, preferred_element_type=jnp.float32)
    inverse = lax.rsqrt(lax.optimization_barrier(jnp.sum(output * output, axis=-1, keepdims=True)) + EPS)
    unit = output * inverse
    return (hidden_pre, hidden, inverse, unit, unit.astype(jnp.bfloat16))

def tower_grads(features, hidden_pre, hidden, inverse, unit, upstream, w_item_out):
    out_grad = (inverse * (upstream - unit * lax.optimization_barrier(jnp.sum(unit * upstream, axis=-1, keepdims=True)))).astype(jnp.bfloat16)
    hidden_grad = jnp.dot(out_grad, w_item_out.T, preferred_element_type=jnp.float32)
    sigma = jax.nn.sigmoid(hidden_pre)
    pre_grad = (hidden_grad * (sigma * (1.0 + hidden_pre * (1.0 - sigma)))).astype(jnp.bfloat16)
    grad_out = jnp.dot(hidden.T, out_grad, preferred_element_type=jnp.float32)
    grad_in = jnp.dot(features.T, pre_grad, preferred_element_type=jnp.float32)
    return (grad_in, grad_out)

def reference(queries, item_table, w_query, w_item_in, w_item_out, pos_owner, pos_rows, neg_owner, neg_rows, neg_logq):
    loss_scale = 1.0 / math.sqrt(QUERIES)
    per_group = QUERIES // GROUPS
    query_blocks = queries.reshape(GROUPS, per_group, QF)
    pos_ids = (pos_owner[:, 0].astype(jnp.int32) * ITEMS_DEV + pos_rows.astype(jnp.int32)).reshape(GROUPS, per_group)
    neg_ids = neg_owner[:, :, 0].astype(jnp.int32) * ITEMS_DEV + neg_rows.astype(jnp.int32)

    def group_step(carry, inputs):
        block, pos_id, neg_id, logq = inputs
        all_ids = jnp.concatenate([neg_id, pos_id]).astype(jnp.int32)
        features = jnp.take(item_table, all_ids, axis=0)
        hidden_pre, hidden, inverse, unit, embed = item_tower(features, w_item_in, w_item_out)
        neg_embed = embed[:NEG]
        pos_embed = embed[NEG:]
        query_pre = jnp.dot(block, w_query, preferred_element_type=jnp.float32)
        query_scale = lax.rsqrt(lax.optimization_barrier(jnp.sum(query_pre * query_pre, axis=-1, keepdims=True)) + EPS)
        query_unit = query_pre * query_scale
        query_embed = query_unit.astype(jnp.bfloat16)
        scores = jnp.dot(query_embed, neg_embed.T, preferred_element_type=jnp.float32)
        logits = scores / TAU - logq[None, :]
        weights_exp = jnp.exp(logits)
        pos_logit = lax.optimization_barrier(jnp.sum(query_embed.astype(jnp.float32) * pos_embed.astype(jnp.float32), axis=-1)) / TAU
        pos_exp = jnp.exp(pos_logit)
        total = pos_exp + lax.optimization_barrier(jnp.sum(weights_exp, axis=-1))
        neg_weight = (loss_scale * weights_exp / total[:, None]).astype(jnp.bfloat16)
        pos_weight = loss_scale * (pos_exp / total - 1.0)
        query_grad = (jnp.dot(neg_weight, neg_embed, preferred_element_type=jnp.float32) + pos_weight[:, None] * pos_embed.astype(jnp.float32)) / TAU
        pre_grad_query = (query_scale * (query_grad - query_unit * lax.optimization_barrier(jnp.sum(query_unit * query_grad, axis=-1, keepdims=True)))).astype(jnp.bfloat16)
        grad_query = jnp.dot(block.T, pre_grad_query, preferred_element_type=jnp.float32)
        neg_grad = jnp.dot(neg_weight.T, query_embed, preferred_element_type=jnp.float32) / TAU
        pos_grad = pos_weight[:, None] * query_embed.astype(jnp.float32) / TAU
        upstream = jnp.concatenate([neg_grad, pos_grad], axis=0)
        grad_in, grad_out = tower_grads(features, hidden_pre, hidden, inverse, unit, upstream, w_item_out)
        return ((carry[0] + grad_query, carry[1] + grad_in, carry[2] + grad_out), None)
    start = (jnp.zeros((QF, E), jnp.float32), jnp.zeros((F, H), jnp.float32), jnp.zeros((H, E), jnp.float32))
    sums, unused = lax.scan(group_step, start, (query_blocks, pos_ids, neg_ids, neg_logq))
    return (sums[0], sums[1], sums[2])
```

```python
import functools
import math

import jax
import jax.numpy as jnp
from jax import lax
from jax.experimental import pallas as pl
from jax.experimental.pallas import tpu as pltpu
from jax.sharding import PartitionSpec as P

TAU = 0.02
EPS = 1e-06
CORES = 2
PARTS = 2
DEPTH = 4


def add_tiles(shape, left, right, out):
    count = math.prod(shape)

    def body(step, carry):
        index = []
        rest = step
        for size in reversed(shape):
            index.insert(0, lax.rem(rest, size))
            rest = lax.div(rest, size)
        index = tuple(index)
        total = left(index)[...].astype(jnp.float32) + right(index)[...].astype(jnp.float32)
        out(index)[...] = total.astype(out(index).dtype)
        return carry

    lax.fori_loop(0, count, body, 0)


def reduce_kernel(
    sizes, grads, out, pair, x_first, y_first, y_second, x_second, held_x, held_y, last, total_a, total_b, send, recv
):
    nx, nz, ny = sizes
    query = lax.axis_index("query")
    item = lax.axis_index("item")
    my_x, my_core = query // CORES, query % CORES
    my_z, my_y = item // ny, item % ny

    def at_core(c):
        return {"query": my_x * CORES + c, "item": item}

    def at_x(x):
        return {"query": x * CORES + my_core, "item": item}

    def at_y(y):
        return {"query": query, "item": my_z * ny + y}

    def at_z(z):
        return {"query": query, "item": z * ny + my_y}

    other = 1 - my_core
    xs = [lax.rem(my_x + d, nx) for d in range(1, nx)]
    ys = [lax.rem(my_y + d, ny) for d in range(1, ny)]
    zs = [lax.rem(my_z + d, nz) for d in range(1, nz)]
    barrier = pltpu.get_barrier_semaphore()
    partners = [at_core(other)] + [at_x(x) for x in xs] + [at_y(y) for y in ys] + [at_z(z) for z in zs]
    for partner in partners:
        pl.semaphore_signal(barrier, inc=1, device_id=partner, device_id_type=pl.DeviceIdType.MESH)
    pl.semaphore_wait(barrier, len(partners))

    used = [0]

    def copy(source, target, partner):
        slot = used[0]
        used[0] += 1
        made = pltpu.make_async_remote_copy(
            src_ref=source,
            dst_ref=target,
            send_sem=send.at[slot],
            recv_sem=recv.at[slot],
            device_id=partner,
            device_id_type=pl.DeviceIdType.MESH,
        )
        made.start()
        return made

    core_copies = [
        copy(grads.at[part, :, other], pair.at[part], at_core(other)) for part in range(PARTS)
    ]

    def core_sum(part):
        core_copies[part].wait_recv()
        add_tiles(
            (nx, nz, ny),
            lambda i: grads.at[part, i[0], my_core, i[1], i[2]],
            lambda i: pair.at[part, i[0], i[1], i[2]],
            lambda i: (held_x if part == 0 else held_y).at[i[0], i[1], i[2]],
        )

    core_sum(0)
    a1 = [copy(held_x.at[x], x_first.at[d], at_x(x)) for d, x in enumerate(xs)]
    core_sum(1)
    b1 = [copy(held_y.at[:, :, y], y_first.at[d], at_y(y)) for d, y in enumerate(ys)]

    for d, made in enumerate(a1):
        made.wait_recv()
        base = (lambda i: held_x.at[my_x, i[0], i[1]]) if d == 0 else (lambda i: pair.at[0, 0, i[0], i[1]])
        add_tiles((nz, ny), base, lambda i, d=d: x_first.at[d, i[0], i[1]], lambda i: pair.at[0, 0, i[0], i[1]])
    a2 = [copy(pair.at[0, 0, :, y], y_second.at[d], at_y(y)) for d, y in enumerate(ys)]

    for d, made in enumerate(b1):
        made.wait_recv()
        base = (lambda i: held_y.at[i[0], i[1], my_y]) if d == 0 else (lambda i: pair.at[1, i[0], i[1], 0])
        add_tiles((nx, nz), base, lambda i, d=d: y_first.at[d, i[0], i[1]], lambda i: pair.at[1, i[0], i[1], 0])
    b2 = [copy(pair.at[1, x, :, 0], x_second.at[d], at_x(x)) for d, x in enumerate(xs)]

    for d, made in enumerate(a2):
        made.wait_recv()
        base = (lambda i: pair.at[0, 0, i[0], my_y]) if d == 0 else (lambda i: total_a.at[i[0]])
        add_tiles((nz,), base, lambda i, d=d: y_second.at[d, i[0]], lambda i: total_a.at[i[0]])
    a3 = [copy(total_a.at[z], last.at[0, d], at_z(z)) for d, z in enumerate(zs)]

    for d, made in enumerate(b2):
        made.wait_recv()
        base = (lambda i: pair.at[1, my_x, i[0], 0]) if d == 0 else (lambda i: total_b.at[i[0]])
        add_tiles((nz,), base, lambda i, d=d: x_second.at[d, i[0]], lambda i: total_b.at[i[0]])
    b3 = [copy(total_b.at[z], last.at[1, d], at_z(z)) for d, z in enumerate(zs)]

    for part, copies, total in ((0, a3, total_a), (1, b3, total_b)):
        for made in copies:
            made.wait_recv()
        result = total[my_z].astype(jnp.float32)
        for d in range(nz - 1):
            result = result + last[part, d].astype(jnp.float32)
        out[part] = result
    for made in core_copies + a1 + b1 + a2 + b2 + a3 + b3:
        made.wait_send()


def reduce_grads(grads, sizes):
    nx, nz, ny = sizes
    rows, width = grads.shape[-2:]
    tile = (rows, width)
    copies = PARTS + 2 * (nx - 1) + 2 * (ny - 1) + 2 * (nz - 1)

    def held(*lead):
        return pltpu.VMEM(lead + tile, jnp.bfloat16)

    return pl.pallas_call(
        functools.partial(reduce_kernel, sizes),
        out_shape=jax.ShapeDtypeStruct((PARTS,) + tile, jnp.float32),
        in_specs=[pl.BlockSpec(memory_space=pltpu.VMEM)],
        out_specs=pl.BlockSpec(memory_space=pltpu.VMEM),
        scratch_shapes=[
            held(PARTS, nx, nz, ny),
            held(nx - 1, nz, ny),
            held(ny - 1, nx, nz),
            held(ny - 1, nz),
            held(nx - 1, nz),
            held(nx, nz, ny),
            held(nx, nz, ny),
            held(PARTS, nz - 1),
            held(nz),
            held(nz),
            pltpu.SemaphoreType.DMA((copies,)),
            pltpu.SemaphoreType.DMA((copies,)),
        ],
        compiler_params=pltpu.CompilerParams(
            collective_id=0, has_side_effects=True, vmem_limit_bytes=40 * 1024 * 1024
        ),
        cost_estimate=pl.CostEstimate(flops=10**7, bytes_accessed=10**8, transcendentals=0),
    )(grads)


def slot_numbers(owners):
    place = jnp.arange(owners.shape[0], dtype=jnp.int32)
    same = (owners[:, None] == owners[None, :]) & (place[:, None] < place[None, :])
    return jnp.sum(same.astype(jnp.int32), axis=0)


def pick(flat, rows):
    onehot = (flat[:, None] == jnp.arange(rows.shape[0], dtype=jnp.int32)[None, :]).astype(
        jnp.bfloat16
    )
    return jnp.dot(onehot, rows, preferred_element_type=jnp.float32).astype(jnp.bfloat16)


def to_slots(flat, values, count):
    hit = flat[:, None] == jnp.arange(count, dtype=jnp.int32)[None, :]
    return jnp.sum(jnp.where(hit, values[:, None], 0), axis=0)


def item_tower(features, w_item_in, w_item_out):
    hidden_pre = jnp.dot(features, w_item_in, preferred_element_type=jnp.float32)
    hidden = jax.nn.silu(hidden_pre).astype(jnp.bfloat16)
    output = jnp.dot(hidden, w_item_out, preferred_element_type=jnp.float32)
    inverse = lax.rsqrt(jnp.sum(output * output, axis=-1, keepdims=True) + EPS)
    unit = output * inverse
    return (hidden_pre, hidden, inverse, unit, unit.astype(jnp.bfloat16))


def tower_grads(features, hidden_pre, hidden, inverse, unit, upstream, w_item_out):
    out_grad = (
        inverse * (upstream - unit * jnp.sum(unit * upstream, axis=-1, keepdims=True))
    ).astype(jnp.bfloat16)
    hidden_grad = lax.dot_general(
        out_grad, w_item_out, (((1,), (1,)), ((), ())), preferred_element_type=jnp.float32
    )
    sigma = jax.nn.sigmoid(hidden_pre)
    pre_grad = (hidden_grad * (sigma * (1.0 + hidden_pre * (1.0 - sigma)))).astype(jnp.bfloat16)
    grad_out = lax.dot_general(
        hidden, out_grad, (((0,), (0,)), ((), ())), preferred_element_type=jnp.float32
    )
    grad_in = lax.dot_general(
        features, pre_grad, (((0,), (0,)), ((), ())), preferred_element_type=jnp.float32
    )
    return (grad_in, grad_out)


def on_device(
    queries,
    item_table,
    w_query,
    w_item_in,
    w_item_out,
    pos_owner,
    pos_rows,
    neg_owner,
    neg_rows,
    neg_logq,
):
    owner_count = lax.axis_size("item")
    query_axis = lax.axis_size("query")
    query_count = queries.shape[0]
    total_queries = query_count * owner_count * query_axis
    loss_scale = 1.0 / math.sqrt(total_queries)
    my_index = lax.axis_index("item")
    negatives = neg_rows.shape[1]
    capacity = 2 * (negatives // owner_count)
    pos_capacity = max(2, 2 * query_count // owner_count)

    pos_owners = pos_owner[:, 0]
    pos_flat = pos_owners * pos_capacity + slot_numbers(pos_owners)
    request = to_slots(pos_flat, pos_rows, owner_count * pos_capacity)
    asked = lax.all_to_all(
        request.reshape(owner_count, pos_capacity), "item", split_axis=0, concat_axis=0, tiled=True
    )
    neg_owners = neg_owner[0, :, 0]
    neg_flat = neg_owners * capacity + slot_numbers(neg_owners)
    own_rows = to_slots(neg_flat - my_index * capacity, neg_rows[0], capacity)

    neg_own = jnp.take(item_table, own_rows, axis=0, mode="clip")
    neg_held = lax.all_gather(neg_own, "item", axis=0, tiled=True)
    pos_own = jnp.take(item_table, asked.reshape(-1), axis=0, mode="clip")
    pos_held = lax.all_to_all(
        pos_own.reshape(owner_count, pos_capacity, -1), "item", split_axis=0, concat_axis=0, tiled=True
    ).reshape(owner_count * pos_capacity, -1)

    query_pre = jnp.dot(queries, w_query, preferred_element_type=jnp.float32)
    query_scale = lax.rsqrt(jnp.sum(query_pre * query_pre, axis=-1, keepdims=True) + EPS)
    query_unit = query_pre * query_scale
    query_embed = query_unit.astype(jnp.bfloat16)

    features = jnp.concatenate([pick(neg_flat, neg_held), pick(pos_flat, pos_held)], axis=0)
    hidden_pre, hidden, inverse, unit, item_embed = item_tower(features, w_item_in, w_item_out)
    neg_embed = item_embed[:negatives]
    pos_embed = item_embed[negatives:]
    scores = lax.dot_general(
        query_embed, neg_embed, (((1,), (1,)), ((), ())), preferred_element_type=jnp.float32
    )
    weights_exp = jnp.exp(scores / TAU - neg_logq)
    pos_logit = (
        jnp.sum(query_embed.astype(jnp.float32) * pos_embed.astype(jnp.float32), axis=-1) / TAU
    )
    pos_exp = jnp.exp(pos_logit)
    total = pos_exp + jnp.sum(weights_exp, axis=-1)
    neg_weight = (loss_scale * weights_exp / total[:, None]).astype(jnp.bfloat16)
    pos_weight = loss_scale * (pos_exp / total - 1.0)
    query_grad = (
        jnp.dot(neg_weight, neg_embed, preferred_element_type=jnp.float32)
        + pos_weight[:, None] * pos_embed.astype(jnp.float32)
    ) / TAU
    pre_grad_query = (
        query_scale
        * (query_grad - query_unit * jnp.sum(query_unit * query_grad, axis=-1, keepdims=True))
    ).astype(jnp.bfloat16)
    grad_query = lax.dot_general(
        queries, pre_grad_query, (((0,), (0,)), ((), ())), preferred_element_type=jnp.float32
    )
    pos_grad = pos_weight[:, None] * query_embed.astype(jnp.float32) / TAU
    neg_grad = (
        lax.dot_general(
            neg_weight, query_embed, (((0,), (0,)), ((), ())), preferred_element_type=jnp.float32
        )
        / TAU
    )
    upstream = jnp.concatenate([neg_grad, pos_grad], axis=0)
    grad_in, grad_out = tower_grads(
        features, hidden_pre, hidden, inverse, unit, upstream, w_item_out
    )

    nz = DEPTH if owner_count % DEPTH == 0 else 1
    ny = owner_count // nz
    nx = query_axis // CORES

    def blocks(grad):
        rows = grad.shape[0] // (owner_count * PARTS)
        split = grad.astype(jnp.bfloat16).reshape(nz, ny, PARTS, rows, nx, CORES, -1)
        return split.transpose(2, 4, 5, 0, 1, 3, 6)

    widths = [grad.shape[1] // query_axis for grad in (grad_query, grad_in, grad_out)]
    grads = jnp.concatenate([blocks(grad_query), blocks(grad_in), blocks(grad_out)], axis=-1)
    summed = reduce_grads(grads, (nx, nz, ny)).reshape(-1, grads.shape[-1])
    return (
        summed[:, : widths[0]],
        summed[:, widths[0] : widths[0] + widths[1]],
        summed[:, widths[0] + widths[1] :],
    )


def solution(mesh):
    return jax.shard_map(
        on_device,
        mesh=mesh,
        in_specs=(
            P(("query", "item"), None),
            P("item", None),
            P(),
            P(),
            P(),
            P(("query", "item"), None),
            P(("query", "item")),
            P("query", None, None),
            P("query", None),
            P("query", None),
        ),
        out_specs=(P("item", "query"), P("item", "query"), P("item", "query")),
        check_vma=False,
    )
```

```python
import functools
import math

import jax
import jax.numpy as jnp
from jax import lax
from jax.experimental import pallas as pl
from jax.experimental.pallas import tpu as pltpu
from jax.sharding import PartitionSpec as P

TAU = 0.02
EPS = 1e-06
CORES = 2
PARTS = 2
DEPTH = 4
TILE = 256


def add_tiles(shape, left, right, out):
    count = math.prod(shape)

    def body(step, carry):
        index = []
        rest = step
        for size in reversed(shape):
            index.insert(0, lax.rem(rest, size))
            rest = lax.div(rest, size)
        index = tuple(index)
        total = left(index)[...].astype(jnp.float32) + right(index)[...].astype(jnp.float32)
        out(index)[...] = total.astype(out(index).dtype)
        return carry

    lax.fori_loop(0, count, body, 0)


def reduce_kernel(
    sizes, queries, features, hidden, query_side, in_side, out_side, out, grads, pair, x_first, y_first, y_second, x_second,
    held_x, held_y, last, total_a, total_b, send, recv
):
    nx, nz, ny = sizes
    query = lax.axis_index("query")
    item = lax.axis_index("item")
    my_x, my_core = query // CORES, query % CORES
    my_z, my_y = item // ny, item % ny

    def at_core(c):
        return {"query": my_x * CORES + c, "item": item}

    def at_x(x):
        return {"query": x * CORES + my_core, "item": item}

    def at_y(y):
        return {"query": query, "item": my_z * ny + y}

    def at_z(z):
        return {"query": query, "item": z * ny + my_y}

    other = 1 - my_core
    xs = [lax.rem(my_x + d, nx) for d in range(1, nx)]
    ys = [lax.rem(my_y + d, ny) for d in range(1, ny)]
    zs = [lax.rem(my_z + d, nz) for d in range(1, nz)]
    barrier = pltpu.get_barrier_semaphore()
    partners = [at_core(other)] + [at_x(x) for x in xs] + [at_y(y) for y in ys] + [at_z(z) for z in zs]
    for partner in partners:
        pl.semaphore_signal(barrier, inc=1, device_id=partner, device_id_type=pl.DeviceIdType.MESH)
    pl.semaphore_wait(barrier, len(partners))

    used = [0]

    def copy(source, target, partner):
        slot = used[0]
        used[0] += 1
        made = pltpu.make_async_remote_copy(
            src_ref=source,
            dst_ref=target,
            send_sem=send.at[slot],
            recv_sem=recv.at[slot],
            device_id=partner,
            device_id_type=pl.DeviceIdType.MESH,
        )
        made.start()
        return made

    rows = grads.shape[-2]
    span = rows * PARTS
    items = TILE // span

    def products(core):
        def body(tile, carry):
            here = pl.ds(pl.multiple_of(tile * TILE, TILE), TILE)
            made = []
            for left, right in ((queries, query_side), (features, in_side), (hidden, out_side)):
                made.append(
                    lax.dot_general(
                        left[:, here],
                        right[core],
                        (((0,), (0,)), ((), ())),
                        preferred_element_type=jnp.float32,
                    ).astype(jnp.bfloat16)
                )
            for x in range(nx):
                block = jnp.concatenate(
                    [m[:, x * (m.shape[1] // nx) : (x + 1) * (m.shape[1] // nx)] for m in made], axis=1
                )
                for j in range(items):
                    place = tile * items + j
                    for part in range(PARTS):
                        start = j * span + part * rows
                        grads[part, x, core, place // ny, place % ny] = block[start : start + rows]
            return carry

        lax.fori_loop(0, queries.shape[1] // TILE, body, 0)

    products(other)
    core_copies = [
        copy(grads.at[part, :, other], pair.at[part], at_core(other)) for part in range(PARTS)
    ]
    products(my_core)

    def core_sum(part):
        core_copies[part].wait_recv()
        add_tiles(
            (nx, nz, ny),
            lambda i: grads.at[part, i[0], my_core, i[1], i[2]],
            lambda i: pair.at[part, i[0], i[1], i[2]],
            lambda i: (held_x if part == 0 else held_y).at[i[0], i[1], i[2]],
        )

    core_sum(0)
    a1 = [copy(held_x.at[x], x_first.at[d], at_x(x)) for d, x in enumerate(xs)]
    core_sum(1)
    b1 = [copy(held_y.at[:, :, y], y_first.at[d], at_y(y)) for d, y in enumerate(ys)]

    for d, made in enumerate(a1):
        made.wait_recv()
        base = (lambda i: held_x.at[my_x, i[0], i[1]]) if d == 0 else (lambda i: pair.at[0, 0, i[0], i[1]])
        add_tiles((nz, ny), base, lambda i, d=d: x_first.at[d, i[0], i[1]], lambda i: pair.at[0, 0, i[0], i[1]])
    a2 = [copy(pair.at[0, 0, :, y], y_second.at[d], at_y(y)) for d, y in enumerate(ys)]

    for d, made in enumerate(b1):
        made.wait_recv()
        base = (lambda i: held_y.at[i[0], i[1], my_y]) if d == 0 else (lambda i: pair.at[1, i[0], i[1], 0])
        add_tiles((nx, nz), base, lambda i, d=d: y_first.at[d, i[0], i[1]], lambda i: pair.at[1, i[0], i[1], 0])
    b2 = [copy(pair.at[1, x, :, 0], x_second.at[d], at_x(x)) for d, x in enumerate(xs)]

    for d, made in enumerate(a2):
        made.wait_recv()
        base = (lambda i: pair.at[0, 0, i[0], my_y]) if d == 0 else (lambda i: total_a.at[i[0]])
        add_tiles((nz,), base, lambda i, d=d: y_second.at[d, i[0]], lambda i: total_a.at[i[0]])
    a3 = [copy(total_a.at[z], last.at[0, d], at_z(z)) for d, z in enumerate(zs)]

    for d, made in enumerate(b2):
        made.wait_recv()
        base = (lambda i: pair.at[1, my_x, i[0], 0]) if d == 0 else (lambda i: total_b.at[i[0]])
        add_tiles((nz,), base, lambda i, d=d: x_second.at[d, i[0]], lambda i: total_b.at[i[0]])
    b3 = [copy(total_b.at[z], last.at[1, d], at_z(z)) for d, z in enumerate(zs)]

    for part, copies, total in ((0, a3, total_a), (1, b3, total_b)):
        for made in copies:
            made.wait_recv()
        result = total[my_z].astype(jnp.float32)
        for d in range(nz - 1):
            result = result + last[part, d].astype(jnp.float32)
        out[part] = result
    for made in core_copies + a1 + b1 + a2 + b2 + a3 + b3:
        made.wait_send()


def reduce_grads(operands, sizes, tile):
    nx, nz, ny = sizes
    copies = PARTS + 2 * (nx - 1) + 2 * (ny - 1) + 2 * (nz - 1)

    def held(*lead):
        return pltpu.VMEM(lead + tile, jnp.bfloat16)

    return pl.pallas_call(
        functools.partial(reduce_kernel, sizes),
        out_shape=jax.ShapeDtypeStruct((PARTS,) + tile, jnp.float32),
        in_specs=[pl.BlockSpec(memory_space=pltpu.VMEM)] * len(operands),
        out_specs=pl.BlockSpec(memory_space=pltpu.VMEM),
        scratch_shapes=[
            held(PARTS, nx, CORES, nz, ny),
            held(PARTS, nx, nz, ny),
            held(nx - 1, nz, ny),
            held(ny - 1, nx, nz),
            held(ny - 1, nz),
            held(nx - 1, nz),
            held(nx, nz, ny),
            held(nx, nz, ny),
            held(PARTS, nz - 1),
            held(nz),
            held(nz),
            pltpu.SemaphoreType.DMA((copies,)),
            pltpu.SemaphoreType.DMA((copies,)),
        ],
        compiler_params=pltpu.CompilerParams(
            collective_id=0, has_side_effects=True, vmem_limit_bytes=40 * 1024 * 1024
        ),
        cost_estimate=pl.CostEstimate(flops=10**10, bytes_accessed=10**7, transcendentals=0),
    )(*operands)


def fetch_kernel(sizes, neg_own, pos_own, neg_out, pos_out, z_send, z_recv, y_send, y_recv, p_send, p_recv):
    nz, ny = sizes
    item_count = nz * ny
    item = lax.axis_index("item")
    my_z, my_y = item // ny, item % ny
    peers = [lax.rem(item + d, item_count) for d in range(1, item_count)]
    barrier = pltpu.get_barrier_semaphore()
    for peer in peers:
        pl.semaphore_signal(
            barrier, inc=1, device_id={"item": peer}, device_id_type=pl.DeviceIdType.MESH
        )
    pl.semaphore_wait(barrier, len(peers))

    def copy(source, target, send, recv, peer):
        return pltpu.make_async_remote_copy(
            src_ref=source,
            dst_ref=target,
            send_sem=send,
            recv_sem=recv,
            device_id={"item": peer},
            device_id_type=pl.DeviceIdType.MESH,
        )

    def along_z(way, step, block):
        source = neg_own if step == 0 else neg_out.at[block * ny + my_y]
        to = (my_z + (1 if way == 0 else -1) + nz) % nz
        return copy(
            source, neg_out.at[block * ny + my_y], z_send.at[way, step], z_recv.at[way, step], to * ny + my_y
        )

    def along_y(way, step, d, block):
        source = neg_own if step == 0 else neg_out.at[block * ny + my_y]
        to = my_z * ny + lax.rem(my_y + d, ny)
        return copy(
            source, neg_out.at[block * ny + my_y], y_send.at[way, step, d - 1], y_recv.at[way, step, d - 1], to
        )

    def from_y(way, step, d, block):
        other = lax.rem(my_y + ny - d, ny)
        return copy(
            neg_own, neg_out.at[block * ny + other], y_send.at[way, step, d - 1], y_recv.at[way, step, d - 1],
            my_z * ny + other,
        )

    def block_at(way, step):
        block = my_z - step if way == 0 else my_z + step
        return block, (block >= 0 if way == 0 else block < nz)

    def has_next(way):
        return my_z < nz - 1 if way == 0 else my_z > 0

    for way in range(2):
        if nz > 1:
            pl.when(has_next(way))(lambda way=way: along_z(way, 0, my_z).start())
    for d in range(1, ny):
        along_y(0, 0, d, my_z).start()
    straight = [
        copy(pos_own.at[peer], pos_out.at[item], p_send.at[d], p_recv.at[d], peer)
        for d, peer in enumerate(peers)
    ]
    for made in straight:
        made.start()
    neg_out[item] = neg_own[...]
    pos_out[item] = pos_own[item]
    for step in range(1, nz):
        for way in range(2):
            block, there = block_at(way, step)

            def arrived(way=way, step=step, block=block):
                along_z(way, step - 1, block).wait_recv()
                if step < nz - 1:
                    pl.when(has_next(way))(lambda: along_z(way, step, block).start())
                for d in range(1, ny):
                    along_y(way, step, d, block).start()

            pl.when(there)(arrived)
    for made in straight:
        made.wait_recv()
    for d in range(1, ny):
        from_y(0, 0, d, my_z).wait_recv()
        along_y(0, 0, d, my_z).wait_send()
    for way in range(2):
        if nz > 1:
            pl.when(has_next(way))(lambda way=way: along_z(way, 0, my_z).wait_send())
        for step in range(1, nz):
            block, there = block_at(way, step)

            def finished(way=way, step=step, block=block):
                if step < nz - 1:
                    pl.when(has_next(way))(lambda: along_z(way, step, block).wait_send())
                for d in range(1, ny):
                    from_y(way, step, d, block).wait_recv()
                    along_y(way, step, d, block).wait_send()

            pl.when(there)(finished)
    for made in straight:
        made.wait_send()


def fetch(neg_own, pos_own, sizes):
    nz, ny = sizes
    item_count = nz * ny
    steps, fans = nz, max(1, ny - 1)
    return pl.pallas_call(
        functools.partial(fetch_kernel, sizes),
        out_shape=(
            jax.ShapeDtypeStruct((item_count,) + neg_own.shape, neg_own.dtype),
            jax.ShapeDtypeStruct(pos_own.shape, pos_own.dtype),
        ),
        in_specs=[pl.BlockSpec(memory_space=pltpu.VMEM)] * 2,
        out_specs=(pl.BlockSpec(memory_space=pltpu.VMEM),) * 2,
        scratch_shapes=[
            pltpu.SemaphoreType.DMA((2, steps)),
            pltpu.SemaphoreType.DMA((2, steps)),
            pltpu.SemaphoreType.DMA((2, steps, fans)),
            pltpu.SemaphoreType.DMA((2, steps, fans)),
            pltpu.SemaphoreType.DMA((item_count - 1,)),
            pltpu.SemaphoreType.DMA((item_count - 1,)),
        ],
        compiler_params=pltpu.CompilerParams(
            collective_id=1, has_side_effects=True, vmem_limit_bytes=32 * 1024 * 1024
        ),
        cost_estimate=pl.CostEstimate(flops=10**6, bytes_accessed=10**8, transcendentals=0),
    )(neg_own, pos_own)


def slot_numbers(owners):
    place = jnp.arange(owners.shape[0], dtype=jnp.int32)
    same = (owners[:, None] == owners[None, :]) & (place[:, None] < place[None, :])
    return jnp.sum(same.astype(jnp.int32), axis=0)


def pick(flat, rows):
    onehot = (flat[:, None] == jnp.arange(rows.shape[0], dtype=jnp.int32)[None, :]).astype(
        jnp.bfloat16
    )
    return jnp.dot(onehot, rows, preferred_element_type=jnp.float32).astype(jnp.bfloat16)


def to_slots(flat, values, count):
    hit = flat[:, None] == jnp.arange(count, dtype=jnp.int32)[None, :]
    return jnp.sum(jnp.where(hit, values[:, None], 0), axis=0)


def item_tower(features, w_item_in, w_item_out):
    hidden_pre = jnp.dot(features, w_item_in, preferred_element_type=jnp.float32)
    hidden = jax.nn.silu(hidden_pre).astype(jnp.bfloat16)
    output = jnp.dot(hidden, w_item_out, preferred_element_type=jnp.float32)
    inverse = lax.rsqrt(jnp.sum(output * output, axis=-1, keepdims=True) + EPS)
    unit = output * inverse
    return (hidden_pre, hidden, inverse, unit, unit.astype(jnp.bfloat16))


def tower_grads(hidden_pre, inverse, unit, upstream, w_item_out):
    out_grad = (
        inverse * (upstream - unit * jnp.sum(unit * upstream, axis=-1, keepdims=True))
    ).astype(jnp.bfloat16)
    hidden_grad = lax.dot_general(
        out_grad, w_item_out, (((1,), (1,)), ((), ())), preferred_element_type=jnp.float32
    )
    sigma = jax.nn.sigmoid(hidden_pre)
    pre_grad = (hidden_grad * (sigma * (1.0 + hidden_pre * (1.0 - sigma)))).astype(jnp.bfloat16)
    return (pre_grad, out_grad)


def on_device(
    queries,
    item_table,
    w_query,
    w_item_in,
    w_item_out,
    pos_owner,
    pos_rows,
    neg_owner,
    neg_rows,
    neg_logq,
):
    owner_count = lax.axis_size("item")
    query_axis = lax.axis_size("query")
    query_count = queries.shape[0]
    total_queries = query_count * owner_count * query_axis
    loss_scale = 1.0 / math.sqrt(total_queries)
    my_index = lax.axis_index("item")
    negatives = neg_rows.shape[1]
    capacity = 2 * (negatives // owner_count)
    pos_capacity = max(2, 2 * query_count // owner_count)

    pos_owners = pos_owner[:, 0]
    pos_flat = pos_owners * pos_capacity + slot_numbers(pos_owners)
    request = to_slots(pos_flat, pos_rows, owner_count * pos_capacity)
    asked = lax.all_to_all(
        request.reshape(owner_count, pos_capacity), "item", split_axis=0, concat_axis=0, tiled=True
    )
    neg_owners = neg_owner[0, :, 0]
    neg_flat = neg_owners * capacity + slot_numbers(neg_owners)
    own_rows = to_slots(neg_flat - my_index * capacity, neg_rows[0], capacity)

    neg_own = jnp.take(item_table, own_rows, axis=0, mode="clip")
    pos_own = jnp.take(item_table, asked.reshape(-1), axis=0, mode="clip")
    nz = DEPTH if owner_count % DEPTH == 0 else 1
    ny = owner_count // nz
    nx = query_axis // CORES
    neg_held, pos_held = fetch(neg_own, pos_own.reshape(owner_count, pos_capacity, -1), (nz, ny))
    neg_held = neg_held.reshape(owner_count * capacity, -1)
    pos_held = pos_held.reshape(owner_count * pos_capacity, -1)

    query_pre = jnp.dot(queries, w_query, preferred_element_type=jnp.float32)
    query_scale = lax.rsqrt(jnp.sum(query_pre * query_pre, axis=-1, keepdims=True) + EPS)
    query_unit = query_pre * query_scale
    query_embed = query_unit.astype(jnp.bfloat16)

    features = jnp.concatenate([pick(neg_flat, neg_held), pick(pos_flat, pos_held)], axis=0)
    hidden_pre, hidden, inverse, unit, item_embed = item_tower(features, w_item_in, w_item_out)
    neg_embed = item_embed[:negatives]
    pos_embed = item_embed[negatives:]
    scores = lax.dot_general(
        query_embed, neg_embed, (((1,), (1,)), ((), ())), preferred_element_type=jnp.float32
    )
    weights_exp = jnp.exp(scores / TAU - neg_logq)
    pos_logit = (
        jnp.sum(query_embed.astype(jnp.float32) * pos_embed.astype(jnp.float32), axis=-1) / TAU
    )
    pos_exp = jnp.exp(pos_logit)
    total = pos_exp + jnp.sum(weights_exp, axis=-1)
    neg_weight = (loss_scale * weights_exp / total[:, None]).astype(jnp.bfloat16)
    pos_weight = loss_scale * (pos_exp / total - 1.0)
    query_grad = (
        jnp.dot(neg_weight, neg_embed, preferred_element_type=jnp.float32)
        + pos_weight[:, None] * pos_embed.astype(jnp.float32)
    ) / TAU
    pre_grad_query = (
        query_scale
        * (query_grad - query_unit * jnp.sum(query_unit * query_grad, axis=-1, keepdims=True))
    ).astype(jnp.bfloat16)
    pos_grad = pos_weight[:, None] * query_embed.astype(jnp.float32) / TAU
    neg_grad = (
        lax.dot_general(
            neg_weight, query_embed, (((0,), (0,)), ((), ())), preferred_element_type=jnp.float32
        )
        / TAU
    )
    upstream = jnp.concatenate([neg_grad, pos_grad], axis=0)
    in_grad, out_grad = tower_grads(hidden_pre, inverse, unit, upstream, w_item_out)

    def by_core(right):
        split = right.reshape(right.shape[0], nx, CORES, -1)
        return split.transpose(2, 0, 1, 3).reshape(CORES, right.shape[0], -1)

    widths = [right.shape[1] // query_axis for right in (pre_grad_query, in_grad, out_grad)]
    tile = (queries.shape[1] // (owner_count * PARTS), sum(widths))
    operands = (queries, features, hidden, by_core(pre_grad_query), by_core(in_grad), by_core(out_grad))
    summed = reduce_grads(operands, (nx, nz, ny), tile).reshape(-1, sum(widths))
    return (
        summed[:, : widths[0]],
        summed[:, widths[0] : widths[0] + widths[1]],
        summed[:, widths[0] + widths[1] :],
    )


def solution(mesh):
    return jax.shard_map(
        on_device,
        mesh=mesh,
        in_specs=(
            P(("query", "item"), None),
            P("item", None),
            P(),
            P(),
            P(),
            P(("query", "item"), None),
            P(("query", "item")),
            P("query", None, None),
            P("query", None),
            P("query", None),
        ),
        out_specs=(P("item", "query"), P("item", "query"), P("item", "query")),
        check_vma=False,
    )
```

```python
import functools
import math

import jax
import jax.numpy as jnp
from jax import lax
from jax.experimental import pallas as pl
from jax.experimental.pallas import tpu as pltpu
from jax.sharding import PartitionSpec as P

TAU = 0.02
EPS = 1e-06
CORES = 2
PARTS = 2
DEPTH = 4
TILE = 256


def add_tiles(shape, left, right, out):
    count = math.prod(shape)

    def body(step, carry):
        index = []
        rest = step
        for size in reversed(shape):
            index.insert(0, lax.rem(rest, size))
            rest = lax.div(rest, size)
        index = tuple(index)
        total = left(index)[...].astype(jnp.float32) + right(index)[...].astype(jnp.float32)
        out(index)[...] = total.astype(out(index).dtype)
        return carry

    lax.fori_loop(0, count, body, 0)


def reduce_kernel(
    sizes, queries, features, hidden, query_side, in_side, out_side, out, grads, pair, x_first, y_first, y_second, x_second,
    held_x, held_y, last, total_a, total_b, send, recv
):
    nx, nz, ny = sizes
    query = lax.axis_index("query")
    item = lax.axis_index("item")
    my_x, my_core = query // CORES, query % CORES
    my_z, my_y = item // ny, item % ny

    def at_core(c):
        return {"query": my_x * CORES + c, "item": item}

    def at_x(x):
        return {"query": x * CORES + my_core, "item": item}

    def at_y(y):
        return {"query": query, "item": my_z * ny + y}

    def at_z(z):
        return {"query": query, "item": z * ny + my_y}

    other = 1 - my_core
    xs = [lax.rem(my_x + d, nx) for d in range(1, nx)]
    ys = [lax.rem(my_y + d, ny) for d in range(1, ny)]
    zs = [lax.rem(my_z + d, nz) for d in range(1, nz)]
    barrier = pltpu.get_barrier_semaphore()
    partners = [at_core(other)] + [at_x(x) for x in xs] + [at_y(y) for y in ys] + [at_z(z) for z in zs]
    for partner in partners:
        pl.semaphore_signal(barrier, inc=1, device_id=partner, device_id_type=pl.DeviceIdType.MESH)
    pl.semaphore_wait(barrier, len(partners))

    used = [0]

    def copy(source, target, partner):
        slot = used[0]
        used[0] += 1
        made = pltpu.make_async_remote_copy(
            src_ref=source,
            dst_ref=target,
            send_sem=send.at[slot],
            recv_sem=recv.at[slot],
            device_id=partner,
            device_id_type=pl.DeviceIdType.MESH,
        )
        made.start()
        return made

    rows = grads.shape[-2]
    span = rows * PARTS
    items = TILE // span

    def side(right, core):
        if len(right.shape) == 3:
            return right[core]
        width = right.shape[1] // (nx * CORES)
        return jnp.concatenate(
            [
                right[:, pl.ds(pl.multiple_of((x * CORES + core) * width, width), width)]
                for x in range(nx)
            ],
            axis=1,
        )

    def products(core):
        def body(tile, carry):
            here = pl.ds(pl.multiple_of(tile * TILE, TILE), TILE)
            made = []
            for left, right in ((queries, query_side), (features, in_side), (hidden, out_side)):
                made.append(
                    lax.dot_general(
                        left[:, here],
                        side(right, core),
                        (((0,), (0,)), ((), ())),
                        preferred_element_type=jnp.float32,
                    ).astype(jnp.bfloat16)
                )
            for x in range(nx):
                block = jnp.concatenate(
                    [m[:, x * (m.shape[1] // nx) : (x + 1) * (m.shape[1] // nx)] for m in made], axis=1
                )
                for j in range(items):
                    place = tile * items + j
                    for part in range(PARTS):
                        start = j * span + part * rows
                        grads[part, x, core, place // ny, place % ny] = block[start : start + rows]
            return carry

        lax.fori_loop(0, queries.shape[1] // TILE, body, 0)

    products(other)
    core_copies = [
        copy(grads.at[part, :, other], pair.at[part], at_core(other)) for part in range(PARTS)
    ]
    products(my_core)

    def core_sum(part):
        core_copies[part].wait_recv()
        add_tiles(
            (nx, nz, ny),
            lambda i: grads.at[part, i[0], my_core, i[1], i[2]],
            lambda i: pair.at[part, i[0], i[1], i[2]],
            lambda i: (held_x if part == 0 else held_y).at[i[0], i[1], i[2]],
        )

    core_sum(0)
    a1 = [copy(held_x.at[x], x_first.at[d], at_x(x)) for d, x in enumerate(xs)]
    core_sum(1)
    b1 = [copy(held_y.at[:, :, y], y_first.at[d], at_y(y)) for d, y in enumerate(ys)]

    for d, made in enumerate(a1):
        made.wait_recv()
        base = (lambda i: held_x.at[my_x, i[0], i[1]]) if d == 0 else (lambda i: pair.at[0, 0, i[0], i[1]])
        add_tiles((nz, ny), base, lambda i, d=d: x_first.at[d, i[0], i[1]], lambda i: pair.at[0, 0, i[0], i[1]])
    a2 = [copy(pair.at[0, 0, :, y], y_second.at[d], at_y(y)) for d, y in enumerate(ys)]

    for d, made in enumerate(b1):
        made.wait_recv()
        base = (lambda i: held_y.at[i[0], i[1], my_y]) if d == 0 else (lambda i: pair.at[1, i[0], i[1], 0])
        add_tiles((nx, nz), base, lambda i, d=d: y_first.at[d, i[0], i[1]], lambda i: pair.at[1, i[0], i[1], 0])
    b2 = [copy(pair.at[1, x, :, 0], x_second.at[d], at_x(x)) for d, x in enumerate(xs)]

    for d, made in enumerate(a2):
        made.wait_recv()
        base = (lambda i: pair.at[0, 0, i[0], my_y]) if d == 0 else (lambda i: total_a.at[i[0]])
        add_tiles((nz,), base, lambda i, d=d: y_second.at[d, i[0]], lambda i: total_a.at[i[0]])
    a3 = [copy(total_a.at[z], last.at[0, d], at_z(z)) for d, z in enumerate(zs)]

    for d, made in enumerate(b2):
        made.wait_recv()
        base = (lambda i: pair.at[1, my_x, i[0], 0]) if d == 0 else (lambda i: total_b.at[i[0]])
        add_tiles((nz,), base, lambda i, d=d: x_second.at[d, i[0]], lambda i: total_b.at[i[0]])
    b3 = [copy(total_b.at[z], last.at[1, d], at_z(z)) for d, z in enumerate(zs)]

    for part, copies, total in ((0, a3, total_a), (1, b3, total_b)):
        for made in copies:
            made.wait_recv()
        result = total[my_z].astype(jnp.float32)
        for d in range(nz - 1):
            result = result + last[part, d].astype(jnp.float32)
        out[part] = result
    for made in core_copies + a1 + b1 + a2 + b2 + a3 + b3:
        made.wait_send()


def reduce_grads(operands, sizes, tile):
    nx, nz, ny = sizes
    copies = PARTS + 2 * (nx - 1) + 2 * (ny - 1) + 2 * (nz - 1)

    def held(*lead):
        return pltpu.VMEM(lead + tile, jnp.bfloat16)

    return pl.pallas_call(
        functools.partial(reduce_kernel, sizes),
        out_shape=jax.ShapeDtypeStruct((PARTS,) + tile, jnp.float32),
        in_specs=[pl.BlockSpec(memory_space=pltpu.VMEM)] * len(operands),
        out_specs=pl.BlockSpec(memory_space=pltpu.VMEM),
        scratch_shapes=[
            held(PARTS, nx, CORES, nz, ny),
            held(PARTS, nx, nz, ny),
            held(nx - 1, nz, ny),
            held(ny - 1, nx, nz),
            held(ny - 1, nz),
            held(nx - 1, nz),
            held(nx, nz, ny),
            held(nx, nz, ny),
            held(PARTS, nz - 1),
            held(nz),
            held(nz),
            pltpu.SemaphoreType.DMA((copies,)),
            pltpu.SemaphoreType.DMA((copies,)),
        ],
        compiler_params=pltpu.CompilerParams(
            collective_id=0, has_side_effects=True, vmem_limit_bytes=40 * 1024 * 1024
        ),
        cost_estimate=pl.CostEstimate(flops=10**10, bytes_accessed=10**7, transcendentals=0),
    )(*operands)


def fetch_kernel(sizes, neg_own, pos_own, neg_out, pos_out, z_send, z_recv, y_send, y_recv, p_send, p_recv):
    nz, ny = sizes
    item_count = nz * ny
    item = lax.axis_index("item")
    my_z, my_y = item // ny, item % ny
    peers = [lax.rem(item + d, item_count) for d in range(1, item_count)]
    barrier = pltpu.get_barrier_semaphore()
    for peer in peers:
        pl.semaphore_signal(
            barrier, inc=1, device_id={"item": peer}, device_id_type=pl.DeviceIdType.MESH
        )
    pl.semaphore_wait(barrier, len(peers))

    def copy(source, target, send, recv, peer):
        return pltpu.make_async_remote_copy(
            src_ref=source,
            dst_ref=target,
            send_sem=send,
            recv_sem=recv,
            device_id={"item": peer},
            device_id_type=pl.DeviceIdType.MESH,
        )

    def along_z(way, step, block):
        source = neg_own if step == 0 else neg_out.at[block * ny + my_y]
        to = (my_z + (1 if way == 0 else -1) + nz) % nz
        return copy(
            source, neg_out.at[block * ny + my_y], z_send.at[way, step], z_recv.at[way, step], to * ny + my_y
        )

    def along_y(way, step, d, block):
        source = neg_own if step == 0 else neg_out.at[block * ny + my_y]
        to = my_z * ny + lax.rem(my_y + d, ny)
        return copy(
            source, neg_out.at[block * ny + my_y], y_send.at[way, step, d - 1], y_recv.at[way, step, d - 1], to
        )

    def from_y(way, step, d, block):
        other = lax.rem(my_y + ny - d, ny)
        return copy(
            neg_own, neg_out.at[block * ny + other], y_send.at[way, step, d - 1], y_recv.at[way, step, d - 1],
            my_z * ny + other,
        )

    def block_at(way, step):
        block = my_z - step if way == 0 else my_z + step
        return block, (block >= 0 if way == 0 else block < nz)

    def has_next(way):
        return my_z < nz - 1 if way == 0 else my_z > 0

    for way in range(2):
        if nz > 1:
            pl.when(has_next(way))(lambda way=way: along_z(way, 0, my_z).start())
    for d in range(1, ny):
        along_y(0, 0, d, my_z).start()
    straight = [
        copy(pos_own.at[peer], pos_out.at[item], p_send.at[d], p_recv.at[d], peer)
        for d, peer in enumerate(peers)
    ]
    neg_out[item] = neg_own[...]
    pos_out[item] = pos_own[item]
    portion = -(-len(straight) // max(1, nz - 1))
    for step in range(1, nz):
        for way in range(2):
            block, there = block_at(way, step)

            def arrived(way=way, step=step, block=block):
                along_z(way, step - 1, block).wait_recv()
                if step < nz - 1:
                    pl.when(has_next(way))(lambda: along_z(way, step, block).start())
                for d in range(1, ny):
                    along_y(way, step, d, block).start()

            pl.when(there)(arrived)
        for made in straight[(step - 1) * portion : step * portion]:
            made.start()
    if nz == 1:
        for made in straight:
            made.start()
    for made in straight:
        made.wait_recv()
    for d in range(1, ny):
        from_y(0, 0, d, my_z).wait_recv()
        along_y(0, 0, d, my_z).wait_send()
    for way in range(2):
        if nz > 1:
            pl.when(has_next(way))(lambda way=way: along_z(way, 0, my_z).wait_send())
        for step in range(1, nz):
            block, there = block_at(way, step)

            def finished(way=way, step=step, block=block):
                if step < nz - 1:
                    pl.when(has_next(way))(lambda: along_z(way, step, block).wait_send())
                for d in range(1, ny):
                    from_y(way, step, d, block).wait_recv()
                    along_y(way, step, d, block).wait_send()

            pl.when(there)(finished)
    for made in straight:
        made.wait_send()


def fetch(neg_own, pos_own, sizes):
    nz, ny = sizes
    item_count = nz * ny
    steps, fans = nz, max(1, ny - 1)
    return pl.pallas_call(
        functools.partial(fetch_kernel, sizes),
        out_shape=(
            jax.ShapeDtypeStruct((item_count,) + neg_own.shape, neg_own.dtype),
            jax.ShapeDtypeStruct(pos_own.shape, pos_own.dtype),
        ),
        in_specs=[pl.BlockSpec(memory_space=pltpu.VMEM)] * 2,
        out_specs=(pl.BlockSpec(memory_space=pltpu.VMEM),) * 2,
        scratch_shapes=[
            pltpu.SemaphoreType.DMA((2, steps)),
            pltpu.SemaphoreType.DMA((2, steps)),
            pltpu.SemaphoreType.DMA((2, steps, fans)),
            pltpu.SemaphoreType.DMA((2, steps, fans)),
            pltpu.SemaphoreType.DMA((item_count - 1,)),
            pltpu.SemaphoreType.DMA((item_count - 1,)),
        ],
        compiler_params=pltpu.CompilerParams(
            collective_id=1, has_side_effects=True, vmem_limit_bytes=32 * 1024 * 1024
        ),
        cost_estimate=pl.CostEstimate(flops=10**6, bytes_accessed=10**8, transcendentals=0),
    )(neg_own, pos_own)


def slot_numbers(owners):
    place = jnp.arange(owners.shape[0], dtype=jnp.int32)
    same = (owners[:, None] == owners[None, :]) & (place[:, None] < place[None, :])
    return jnp.sum(same.astype(jnp.int32), axis=0)


def pick(flat, rows):
    onehot = (flat[:, None] == jnp.arange(rows.shape[0], dtype=jnp.int32)[None, :]).astype(
        jnp.bfloat16
    )
    return jnp.dot(onehot, rows, preferred_element_type=jnp.float32).astype(jnp.bfloat16)


def to_slots(flat, values, count):
    hit = flat[:, None] == jnp.arange(count, dtype=jnp.int32)[None, :]
    return jnp.sum(jnp.where(hit, values[:, None], 0), axis=0)


def item_tower(features, w_item_in, w_item_out):
    hidden_pre = jnp.dot(features, w_item_in, preferred_element_type=jnp.float32)
    hidden = jax.nn.silu(hidden_pre).astype(jnp.bfloat16)
    output = jnp.dot(hidden, w_item_out, preferred_element_type=jnp.float32)
    inverse = lax.rsqrt(jnp.sum(output * output, axis=-1, keepdims=True) + EPS)
    unit = output * inverse
    return (hidden_pre, hidden, inverse, unit, unit.astype(jnp.bfloat16))


def tower_grads(hidden_pre, inverse, unit, upstream, w_item_out):
    out_grad = (
        inverse * (upstream - unit * jnp.sum(unit * upstream, axis=-1, keepdims=True))
    ).astype(jnp.bfloat16)
    hidden_grad = lax.dot_general(
        out_grad, w_item_out, (((1,), (1,)), ((), ())), preferred_element_type=jnp.float32
    )
    sigma = jax.nn.sigmoid(hidden_pre)
    pre_grad = (hidden_grad * (sigma * (1.0 + hidden_pre * (1.0 - sigma)))).astype(jnp.bfloat16)
    return (pre_grad, out_grad)


def on_device(
    queries,
    item_table,
    w_query,
    w_item_in,
    w_item_out,
    pos_owner,
    pos_rows,
    neg_owner,
    neg_rows,
    neg_logq,
):
    owner_count = lax.axis_size("item")
    query_axis = lax.axis_size("query")
    query_count = queries.shape[0]
    total_queries = query_count * owner_count * query_axis
    loss_scale = 1.0 / math.sqrt(total_queries)
    my_index = lax.axis_index("item")
    negatives = neg_rows.shape[1]
    capacity = 2 * (negatives // owner_count)
    pos_capacity = max(2, 2 * query_count // owner_count)

    pos_owners = pos_owner[:, 0]
    pos_flat = pos_owners * pos_capacity + slot_numbers(pos_owners)
    request = to_slots(pos_flat, pos_rows, owner_count * pos_capacity)
    asked = lax.all_to_all(
        request.reshape(owner_count, pos_capacity), "item", split_axis=0, concat_axis=0, tiled=True
    )
    neg_owners = neg_owner[0, :, 0]
    neg_flat = neg_owners * capacity + slot_numbers(neg_owners)
    own_rows = to_slots(neg_flat - my_index * capacity, neg_rows[0], capacity)

    neg_own = jnp.take(item_table, own_rows, axis=0, mode="clip")
    pos_own = jnp.take(item_table, asked.reshape(-1), axis=0, mode="clip")
    nz = DEPTH if owner_count % DEPTH == 0 else 1
    ny = owner_count // nz
    nx = query_axis // CORES
    neg_held, pos_held = fetch(neg_own, pos_own.reshape(owner_count, pos_capacity, -1), (nz, ny))
    neg_held = neg_held.reshape(owner_count * capacity, -1)
    pos_held = pos_held.reshape(owner_count * pos_capacity, -1)

    query_pre = jnp.dot(queries, w_query, preferred_element_type=jnp.float32)
    query_scale = lax.rsqrt(jnp.sum(query_pre * query_pre, axis=-1, keepdims=True) + EPS)
    query_unit = query_pre * query_scale
    query_embed = query_unit.astype(jnp.bfloat16)

    features = jnp.concatenate([pick(neg_flat, neg_held), pick(pos_flat, pos_held)], axis=0)
    hidden_pre, hidden, inverse, unit, item_embed = item_tower(features, w_item_in, w_item_out)
    neg_embed = item_embed[:negatives]
    pos_embed = item_embed[negatives:]
    scores = lax.dot_general(
        query_embed, neg_embed, (((1,), (1,)), ((), ())), preferred_element_type=jnp.float32
    )
    weights_exp = jnp.exp(scores / TAU - neg_logq)
    pos_logit = (
        jnp.sum(query_embed.astype(jnp.float32) * pos_embed.astype(jnp.float32), axis=-1) / TAU
    )
    pos_exp = jnp.exp(pos_logit)
    total = pos_exp + jnp.sum(weights_exp, axis=-1)
    neg_weight = (loss_scale * weights_exp / total[:, None]).astype(jnp.bfloat16)
    pos_weight = loss_scale * (pos_exp / total - 1.0)
    query_grad = (
        jnp.dot(neg_weight, neg_embed, preferred_element_type=jnp.float32)
        + pos_weight[:, None] * pos_embed.astype(jnp.float32)
    ) / TAU
    pre_grad_query = (
        query_scale
        * (query_grad - query_unit * jnp.sum(query_unit * query_grad, axis=-1, keepdims=True))
    ).astype(jnp.bfloat16)
    pos_grad = pos_weight[:, None] * query_embed.astype(jnp.float32) / TAU
    neg_grad = (
        lax.dot_general(
            neg_weight, query_embed, (((0,), (0,)), ((), ())), preferred_element_type=jnp.float32
        )
        / TAU
    )
    upstream = jnp.concatenate([neg_grad, pos_grad], axis=0)
    in_grad, out_grad = tower_grads(hidden_pre, inverse, unit, upstream, w_item_out)

    def by_core(right):
        if right.shape[1] // query_axis % 128 == 0:
            return right
        split = right.reshape(right.shape[0], nx, CORES, -1)
        return split.transpose(2, 0, 1, 3).reshape(CORES, right.shape[0], -1)

    widths = [right.shape[1] // query_axis for right in (pre_grad_query, in_grad, out_grad)]
    tile = (queries.shape[1] // (owner_count * PARTS), sum(widths))
    operands = (queries, features, hidden, by_core(pre_grad_query), by_core(in_grad), by_core(out_grad))
    summed = reduce_grads(operands, (nx, nz, ny), tile).reshape(-1, sum(widths))
    return (
        summed[:, : widths[0]],
        summed[:, widths[0] : widths[0] + widths[1]],
        summed[:, widths[0] + widths[1] :],
    )


def solution(mesh):
    return jax.shard_map(
        on_device,
        mesh=mesh,
        in_specs=(
            P(("query", "item"), None),
            P("item", None),
            P(),
            P(),
            P(),
            P(("query", "item"), None),
            P(("query", "item")),
            P("query", None, None),
            P("query", None),
            P("query", None),
        ),
        out_specs=(P("item", "query"), P("item", "query"), P("item", "query")),
        check_vma=False,
    )
```

```python
import functools
import math

import jax
import jax.numpy as jnp
from jax import lax
from jax.experimental import pallas as pl
from jax.experimental.pallas import tpu as pltpu
from jax.sharding import PartitionSpec as P

TAU = 0.02
EPS = 1e-06
CORES = 2
PARTS = 2
DEPTH = 4
TILE = 256
HALVES = 2


def add_tiles(shape, left, right, out):
    count = math.prod(shape)

    def body(step, carry):
        index = []
        rest = step
        for size in reversed(shape):
            index.insert(0, lax.rem(rest, size))
            rest = lax.div(rest, size)
        index = tuple(index)
        total = left(index)[...].astype(jnp.float32) + right(index)[...].astype(jnp.float32)
        out(index)[...] = total.astype(out(index).dtype)
        return carry

    lax.fori_loop(0, count, body, 0)


def reduce_kernel(
    sizes, queries, features, hidden, query_side, in_side, out_side, out, grads, pair, x_first, y_first, y_second, x_second,
    held_x, held_y, last, total_a, total_b, send, recv
):
    nx, nz, ny = sizes
    query = lax.axis_index("query")
    item = lax.axis_index("item")
    my_x, my_core = query // CORES, query % CORES
    my_z, my_y = item // ny, item % ny

    def at_core(c):
        return {"query": my_x * CORES + c, "item": item}

    def at_x(x):
        return {"query": x * CORES + my_core, "item": item}

    def at_y(y):
        return {"query": query, "item": my_z * ny + y}

    def at_z(z):
        return {"query": query, "item": z * ny + my_y}

    other = 1 - my_core
    xs = [lax.rem(my_x + d, nx) for d in range(1, nx)]
    ys = [lax.rem(my_y + d, ny) for d in range(1, ny)]
    zs = [lax.rem(my_z + d, nz) for d in range(1, nz)]
    barrier = pltpu.get_barrier_semaphore()
    partners = [at_core(other)] + [at_x(x) for x in xs] + [at_y(y) for y in ys] + [at_z(z) for z in zs]
    for partner in partners:
        pl.semaphore_signal(barrier, inc=1, device_id=partner, device_id_type=pl.DeviceIdType.MESH)
    pl.semaphore_wait(barrier, len(partners))

    used = [0]

    def copy(source, target, partner):
        slot = used[0]
        used[0] += 1
        made = pltpu.make_async_remote_copy(
            src_ref=source,
            dst_ref=target,
            send_sem=send.at[slot],
            recv_sem=recv.at[slot],
            device_id=partner,
            device_id_type=pl.DeviceIdType.MESH,
        )
        made.start()
        return made

    rows = grads.shape[-2]
    span = rows * PARTS
    items = TILE // span

    def side(right, core):
        if len(right.shape) == 3:
            return right[core]
        width = right.shape[1] // (nx * CORES)
        return jnp.concatenate(
            [
                right[:, pl.ds(pl.multiple_of((x * CORES + core) * width, width), width)]
                for x in range(nx)
            ],
            axis=1,
        )

    def products(core):
        def body(tile, carry):
            here = pl.ds(pl.multiple_of(tile * TILE, TILE), TILE)
            made = []
            for left, right in ((queries, query_side), (features, in_side), (hidden, out_side)):
                made.append(
                    lax.dot_general(
                        left[:, here],
                        side(right, core),
                        (((0,), (0,)), ((), ())),
                        preferred_element_type=jnp.float32,
                    ).astype(jnp.bfloat16)
                )
            for x in range(nx):
                block = jnp.concatenate(
                    [m[:, x * (m.shape[1] // nx) : (x + 1) * (m.shape[1] // nx)] for m in made], axis=1
                )
                for j in range(items):
                    place = tile * items + j
                    for part in range(PARTS):
                        start = j * span + part * rows
                        grads[part, x, core, place // ny, place % ny] = block[start : start + rows]
            return carry

        lax.fori_loop(0, queries.shape[1] // TILE, body, 0)

    products(other)
    core_copies = [
        copy(grads.at[part, :, other], pair.at[part], at_core(other)) for part in range(PARTS)
    ]
    products(my_core)

    def core_sum(part):
        core_copies[part].wait_recv()
        add_tiles(
            (nx, nz, ny),
            lambda i: grads.at[part, i[0], my_core, i[1], i[2]],
            lambda i: pair.at[part, i[0], i[1], i[2]],
            lambda i: (held_x if part == 0 else held_y).at[i[0], i[1], i[2]],
        )

    core_sum(0)
    a1 = [copy(held_x.at[x], x_first.at[d], at_x(x)) for d, x in enumerate(xs)]
    core_sum(1)
    b1 = [copy(held_y.at[:, :, y], y_first.at[d], at_y(y)) for d, y in enumerate(ys)]

    for d, made in enumerate(a1):
        made.wait_recv()
        base = (lambda i: held_x.at[my_x, i[0], i[1]]) if d == 0 else (lambda i: pair.at[0, 0, i[0], i[1]])
        add_tiles((nz, ny), base, lambda i, d=d: x_first.at[d, i[0], i[1]], lambda i: pair.at[0, 0, i[0], i[1]])
    a2 = [copy(pair.at[0, 0, :, y], y_second.at[d], at_y(y)) for d, y in enumerate(ys)]

    for d, made in enumerate(b1):
        made.wait_recv()
        base = (lambda i: held_y.at[i[0], i[1], my_y]) if d == 0 else (lambda i: pair.at[1, i[0], i[1], 0])
        add_tiles((nx, nz), base, lambda i, d=d: y_first.at[d, i[0], i[1]], lambda i: pair.at[1, i[0], i[1], 0])
    b2 = [copy(pair.at[1, x, :, 0], x_second.at[d], at_x(x)) for d, x in enumerate(xs)]

    for d, made in enumerate(a2):
        made.wait_recv()
        base = (lambda i: pair.at[0, 0, i[0], my_y]) if d == 0 else (lambda i: total_a.at[i[0]])
        add_tiles((nz,), base, lambda i, d=d: y_second.at[d, i[0]], lambda i: total_a.at[i[0]])
    a3 = [copy(total_a.at[z], last.at[0, d], at_z(z)) for d, z in enumerate(zs)]

    for d, made in enumerate(b2):
        made.wait_recv()
        base = (lambda i: pair.at[1, my_x, i[0], 0]) if d == 0 else (lambda i: total_b.at[i[0]])
        add_tiles((nz,), base, lambda i, d=d: x_second.at[d, i[0]], lambda i: total_b.at[i[0]])
    b3 = [copy(total_b.at[z], last.at[1, d], at_z(z)) for d, z in enumerate(zs)]

    for part, copies, total in ((0, a3, total_a), (1, b3, total_b)):
        for made in copies:
            made.wait_recv()
        result = total[my_z].astype(jnp.float32)
        for d in range(nz - 1):
            result = result + last[part, d].astype(jnp.float32)
        out[part] = result
    for made in core_copies + a1 + b1 + a2 + b2 + a3 + b3:
        made.wait_send()


def reduce_grads(operands, sizes, tile):
    nx, nz, ny = sizes
    copies = PARTS + 2 * (nx - 1) + 2 * (ny - 1) + 2 * (nz - 1)

    def held(*lead):
        return pltpu.VMEM(lead + tile, jnp.bfloat16)

    return pl.pallas_call(
        functools.partial(reduce_kernel, sizes),
        out_shape=jax.ShapeDtypeStruct((PARTS,) + tile, jnp.float32),
        in_specs=[pl.BlockSpec(memory_space=pltpu.VMEM)] * len(operands),
        out_specs=pl.BlockSpec(memory_space=pltpu.VMEM),
        scratch_shapes=[
            held(PARTS, nx, CORES, nz, ny),
            held(PARTS, nx, nz, ny),
            held(nx - 1, nz, ny),
            held(ny - 1, nx, nz),
            held(ny - 1, nz),
            held(nx - 1, nz),
            held(nx, nz, ny),
            held(nx, nz, ny),
            held(PARTS, nz - 1),
            held(nz),
            held(nz),
            pltpu.SemaphoreType.DMA((copies,)),
            pltpu.SemaphoreType.DMA((copies,)),
        ],
        compiler_params=pltpu.CompilerParams(
            collective_id=0, has_side_effects=True, vmem_limit_bytes=40 * 1024 * 1024
        ),
        cost_estimate=pl.CostEstimate(flops=10**10, bytes_accessed=10**7, transcendentals=0),
    )(*operands)


def fetch_kernel(sizes, neg_own, pos_own, neg_out, pos_out, z_send, z_recv, y_send, y_recv, p_send, p_recv):
    nz, ny = sizes
    item_count = nz * ny
    item = lax.axis_index("item")
    my_z, my_y = item // ny, item % ny
    peers = [lax.rem(item + d, item_count) for d in range(1, item_count)]
    barrier = pltpu.get_barrier_semaphore()
    for peer in peers:
        pl.semaphore_signal(
            barrier, inc=1, device_id={"item": peer}, device_id_type=pl.DeviceIdType.MESH
        )
    pl.semaphore_wait(barrier, len(peers))

    def copy(source, target, send, recv, peer):
        return pltpu.make_async_remote_copy(
            src_ref=source,
            dst_ref=target,
            send_sem=send,
            recv_sem=recv,
            device_id={"item": peer},
            device_id_type=pl.DeviceIdType.MESH,
        )

    size = neg_own.shape[0] // HALVES

    def source_of(step, block, half):
        rows = pl.ds(half * size, size)
        return neg_own.at[rows] if step == 0 else neg_out.at[block * ny + my_y, rows]

    def along_z(way, step, block, half):
        to = (my_z + (1 if way == 0 else -1) + nz) % nz
        return copy(
            source_of(step, block, half),
            neg_out.at[block * ny + my_y, pl.ds(half * size, size)],
            z_send.at[way, step, half],
            z_recv.at[way, step, half],
            to * ny + my_y,
        )

    def along_y(way, step, d, block, half):
        return copy(
            source_of(step, block, half),
            neg_out.at[block * ny + my_y, pl.ds(half * size, size)],
            y_send.at[way, step, d - 1, half],
            y_recv.at[way, step, d - 1, half],
            my_z * ny + lax.rem(my_y + d, ny),
        )

    def from_y(way, step, d, block, half):
        other = lax.rem(my_y + ny - d, ny)
        rows = pl.ds(half * size, size)
        return copy(
            neg_own.at[rows],
            neg_out.at[block * ny + other, rows],
            y_send.at[way, step, d - 1, half],
            y_recv.at[way, step, d - 1, half],
            my_z * ny + other,
        )

    def block_at(way, step):
        block = my_z - step if way == 0 else my_z + step
        return block, (block >= 0 if way == 0 else block < nz)

    def has_next(way):
        return my_z < nz - 1 if way == 0 else my_z > 0

    for half in range(HALVES):
        for way in range(2):
            if nz > 1:
                pl.when(has_next(way))(lambda way=way, half=half: along_z(way, 0, my_z, half).start())
        for d in range(1, ny):
            along_y(0, 0, d, my_z, half).start()
    straight = [
        copy(pos_own.at[peer], pos_out.at[item], p_send.at[d], p_recv.at[d], peer)
        for d, peer in enumerate(peers)
    ]
    neg_out[item] = neg_own[...]
    pos_out[item] = pos_own[item]
    stages = max(1, (nz - 1) * HALVES)
    bounds = [len(straight) * k // stages for k in range(stages + 1)]
    for step in range(1, nz):
        for half in range(HALVES):
            for way in range(2):
                block, there = block_at(way, step)

                def arrived(way=way, step=step, block=block, half=half):
                    along_z(way, step - 1, block, half).wait_recv()
                    if step < nz - 1:
                        pl.when(has_next(way))(lambda: along_z(way, step, block, half).start())
                    for d in range(1, ny):
                        along_y(way, step, d, block, half).start()

                pl.when(there)(arrived)
            stage = (step - 1) * HALVES + half
            for made in straight[bounds[stage] : bounds[stage + 1]]:
                made.start()
    if nz == 1:
        for made in straight:
            made.start()
    for made in straight:
        made.wait_recv()
    for half in range(HALVES):
        for d in range(1, ny):
            from_y(0, 0, d, my_z, half).wait_recv()
            along_y(0, 0, d, my_z, half).wait_send()
        for way in range(2):
            if nz > 1:
                pl.when(has_next(way))(
                    lambda way=way, half=half: along_z(way, 0, my_z, half).wait_send()
                )
            for step in range(1, nz):
                block, there = block_at(way, step)

                def finished(way=way, step=step, block=block, half=half):
                    if step < nz - 1:
                        pl.when(has_next(way))(lambda: along_z(way, step, block, half).wait_send())
                    for d in range(1, ny):
                        from_y(way, step, d, block, half).wait_recv()
                        along_y(way, step, d, block, half).wait_send()

                pl.when(there)(finished)
    for made in straight:
        made.wait_send()


def fetch(neg_own, pos_own, sizes):
    nz, ny = sizes
    item_count = nz * ny
    steps, fans = nz, max(1, ny - 1)
    return pl.pallas_call(
        functools.partial(fetch_kernel, sizes),
        out_shape=(
            jax.ShapeDtypeStruct((item_count,) + neg_own.shape, neg_own.dtype),
            jax.ShapeDtypeStruct(pos_own.shape, pos_own.dtype),
        ),
        in_specs=[pl.BlockSpec(memory_space=pltpu.VMEM)] * 2,
        out_specs=(pl.BlockSpec(memory_space=pltpu.VMEM),) * 2,
        scratch_shapes=[
            pltpu.SemaphoreType.DMA((2, steps, HALVES)),
            pltpu.SemaphoreType.DMA((2, steps, HALVES)),
            pltpu.SemaphoreType.DMA((2, steps, fans, HALVES)),
            pltpu.SemaphoreType.DMA((2, steps, fans, HALVES)),
            pltpu.SemaphoreType.DMA((item_count - 1,)),
            pltpu.SemaphoreType.DMA((item_count - 1,)),
        ],
        compiler_params=pltpu.CompilerParams(
            collective_id=1, has_side_effects=True, vmem_limit_bytes=32 * 1024 * 1024
        ),
        cost_estimate=pl.CostEstimate(flops=10**6, bytes_accessed=10**8, transcendentals=0),
    )(neg_own, pos_own)


def slot_numbers(owners):
    place = jnp.arange(owners.shape[0], dtype=jnp.int32)
    same = (owners[:, None] == owners[None, :]) & (place[:, None] < place[None, :])
    return jnp.sum(same.astype(jnp.int32), axis=0)


def pick(flat, rows):
    onehot = (flat[:, None] == jnp.arange(rows.shape[0], dtype=jnp.int32)[None, :]).astype(
        jnp.bfloat16
    )
    return jnp.dot(onehot, rows, preferred_element_type=jnp.float32).astype(jnp.bfloat16)


def to_slots(flat, values, count):
    hit = flat[:, None] == jnp.arange(count, dtype=jnp.int32)[None, :]
    return jnp.sum(jnp.where(hit, values[:, None], 0), axis=0)


def item_tower(features, w_item_in, w_item_out):
    hidden_pre = jnp.dot(features, w_item_in, preferred_element_type=jnp.float32)
    hidden = jax.nn.silu(hidden_pre).astype(jnp.bfloat16)
    output = jnp.dot(hidden, w_item_out, preferred_element_type=jnp.float32)
    inverse = lax.rsqrt(jnp.sum(output * output, axis=-1, keepdims=True) + EPS)
    unit = output * inverse
    return (hidden_pre, hidden, inverse, unit, unit.astype(jnp.bfloat16))


def tower_grads(hidden_pre, inverse, unit, upstream, w_item_out):
    out_grad = (
        inverse * (upstream - unit * jnp.sum(unit * upstream, axis=-1, keepdims=True))
    ).astype(jnp.bfloat16)
    hidden_grad = lax.dot_general(
        out_grad, w_item_out, (((1,), (1,)), ((), ())), preferred_element_type=jnp.float32
    )
    sigma = jax.nn.sigmoid(hidden_pre)
    pre_grad = (hidden_grad * (sigma * (1.0 + hidden_pre * (1.0 - sigma)))).astype(jnp.bfloat16)
    return (pre_grad, out_grad)


def on_device(
    queries,
    item_table,
    w_query,
    w_item_in,
    w_item_out,
    pos_owner,
    pos_rows,
    neg_owner,
    neg_rows,
    neg_logq,
):
    owner_count = lax.axis_size("item")
    query_axis = lax.axis_size("query")
    query_count = queries.shape[0]
    total_queries = query_count * owner_count * query_axis
    loss_scale = 1.0 / math.sqrt(total_queries)
    my_index = lax.axis_index("item")
    negatives = neg_rows.shape[1]
    capacity = 2 * (negatives // owner_count)
    pos_capacity = max(2, 2 * query_count // owner_count)

    pos_owners = pos_owner[:, 0]
    pos_flat = pos_owners * pos_capacity + slot_numbers(pos_owners)
    request = to_slots(pos_flat, pos_rows, owner_count * pos_capacity)
    asked = lax.all_to_all(
        request.reshape(owner_count, pos_capacity), "item", split_axis=0, concat_axis=0, tiled=True
    )
    neg_owners = neg_owner[0, :, 0]
    neg_flat = neg_owners * capacity + slot_numbers(neg_owners)
    own_rows = to_slots(neg_flat - my_index * capacity, neg_rows[0], capacity)

    neg_own = jnp.take(item_table, own_rows, axis=0, mode="clip")
    pos_own = jnp.take(item_table, asked.reshape(-1), axis=0, mode="clip")
    nz = DEPTH if owner_count % DEPTH == 0 else 1
    ny = owner_count // nz
    nx = query_axis // CORES
    neg_held, pos_held = fetch(neg_own, pos_own.reshape(owner_count, pos_capacity, -1), (nz, ny))
    neg_held = neg_held.reshape(owner_count * capacity, -1)
    pos_held = pos_held.reshape(owner_count * pos_capacity, -1)

    query_pre = jnp.dot(queries, w_query, preferred_element_type=jnp.float32)
    query_scale = lax.rsqrt(jnp.sum(query_pre * query_pre, axis=-1, keepdims=True) + EPS)
    query_unit = query_pre * query_scale
    query_embed = query_unit.astype(jnp.bfloat16)

    features = jnp.concatenate([pick(neg_flat, neg_held), pick(pos_flat, pos_held)], axis=0)
    hidden_pre, hidden, inverse, unit, item_embed = item_tower(features, w_item_in, w_item_out)
    neg_embed = item_embed[:negatives]
    pos_embed = item_embed[negatives:]
    scores = lax.dot_general(
        query_embed, neg_embed, (((1,), (1,)), ((), ())), preferred_element_type=jnp.float32
    )
    weights_exp = jnp.exp(scores / TAU - neg_logq)
    pos_logit = (
        jnp.sum(query_embed.astype(jnp.float32) * pos_embed.astype(jnp.float32), axis=-1) / TAU
    )
    pos_exp = jnp.exp(pos_logit)
    total = pos_exp + jnp.sum(weights_exp, axis=-1)
    neg_weight = (loss_scale * weights_exp / total[:, None]).astype(jnp.bfloat16)
    pos_weight = loss_scale * (pos_exp / total - 1.0)
    query_grad = (
        jnp.dot(neg_weight, neg_embed, preferred_element_type=jnp.float32)
        + pos_weight[:, None] * pos_embed.astype(jnp.float32)
    ) / TAU
    pre_grad_query = (
        query_scale
        * (query_grad - query_unit * jnp.sum(query_unit * query_grad, axis=-1, keepdims=True))
    ).astype(jnp.bfloat16)
    pos_grad = pos_weight[:, None] * query_embed.astype(jnp.float32) / TAU
    neg_grad = (
        lax.dot_general(
            neg_weight, query_embed, (((0,), (0,)), ((), ())), preferred_element_type=jnp.float32
        )
        / TAU
    )
    upstream = jnp.concatenate([neg_grad, pos_grad], axis=0)
    in_grad, out_grad = tower_grads(hidden_pre, inverse, unit, upstream, w_item_out)

    def by_core(right):
        if right.shape[1] // query_axis % 128 == 0:
            return right
        split = right.reshape(right.shape[0], nx, CORES, -1)
        return split.transpose(2, 0, 1, 3).reshape(CORES, right.shape[0], -1)

    widths = [right.shape[1] // query_axis for right in (pre_grad_query, in_grad, out_grad)]
    tile = (queries.shape[1] // (owner_count * PARTS), sum(widths))
    operands = (queries, features, hidden, by_core(pre_grad_query), by_core(in_grad), by_core(out_grad))
    summed = reduce_grads(operands, (nx, nz, ny), tile).reshape(-1, sum(widths))
    return (
        summed[:, : widths[0]],
        summed[:, widths[0] : widths[0] + widths[1]],
        summed[:, widths[0] + widths[1] :],
    )


def solution(mesh):
    return jax.shard_map(
        on_device,
        mesh=mesh,
        in_specs=(
            P(("query", "item"), None),
            P("item", None),
            P(),
            P(),
            P(),
            P(("query", "item"), None),
            P(("query", "item")),
            P("query", None, None),
            P("query", None),
            P("query", None),
        ),
        out_specs=(P("item", "query"), P("item", "query"), P("item", "query")),
        check_vma=False,
    )
```
